32 devices in a mesh: head: 4 (over y, x), inner: 4 (over z), outer: 2 (over core).
Axes of the slice: x: 2, y: 2, z: 4, core: 2. Of those that a mesh axis runs over, the one named last changes fastest.
Arguments:
- queries: bfloat16 [2048, 4096], P(('head', 'inner', 'outer')), may hold values from -9 to 9
- keys: bfloat16 [2048, 512], P(('head', 'inner', 'outer')), may hold values from -6 to 6
- values: bfloat16 [2048, 512], P(('head', 'inner', 'outer')), may hold values from -6 to 6
- grad_out: bfloat16 [2048, 4096], P(('head', 'inner', 'outer')), may hold values from -6 to 6
- block_order: int32 [32], replicated, may hold values from 0 to 31, as said below
Outputs:
- query_grad: bfloat16 [2048, 4096], P(('head', 'inner', 'outer'))
- key_grad: bfloat16 [2048, 512], P(('head', 'inner', 'outer'))
- value_grad: bfloat16 [2048, 512], P(('head', 'inner', 'outer'))
The draws below stay inside these ranges and needn't reach their ends.
Inputs may be any that keep to these rules, and one draw needn't show every extreme that they name: `block_order`: each value appears once. For each r below 8, the values at b = r, 8 + r, ..., 24 + r are, in some order, j_k + 2 k * 8 and 2 (k + 1) * 8 - 1 - j_k for each k below 2, with j_k below 8.
All inputs are finite; a program needn't handle non-finite values.
Results may differ from the reference program's by a relative error of at most 0.033.
Values may be sent and summed in bfloat16 or wider, within the bound.
No kernel may reach another device: no remote copies, remote signals or barrier semaphores. Data moves between devices by JAX's collectives and lax.ppermute only.
A program may use at most 64 MiB of HBM per device.

```python
import jax
import jax.numpy as jnp
from jax import lax

TOK_DEV = 64
HEADS = 32
KV_HEADS = 4
HEAD_DIM = 128
RANKS = 8
BLOCKS = 32
TOKENS = 2048
N_HEAD = 4


def draw_keys(key, part):
    folded = jax.random.fold_in(key, 21)
    base = jnp.clip(jax.random.normal(folded, (TOKENS, KV_HEADS, HEAD_DIM), jnp.float32), -6.0, 6.0)
    return base.reshape(TOKENS, KV_HEADS * HEAD_DIM).astype(jnp.bfloat16)


def draw_queries(key, part):
    folded = jax.random.fold_in(key, 22)
    group_size = HEADS // KV_HEADS
    base = jnp.clip(jax.random.normal(folded, (TOKENS, KV_HEADS, group_size, HEAD_DIM), jnp.float32), -6.0, 6.0)
    return base.reshape(TOKENS, HEADS * HEAD_DIM).astype(jnp.bfloat16)


def draw_block_order(key, part):
    key = jax.random.fold_in(key, 5)
    pair_key, order_key = jax.random.split(key)
    columns = []
    for level in range(N_HEAD // 2):
        chosen = jax.random.permutation(jax.random.fold_in(pair_key, level), RANKS).astype(jnp.int32)
        columns.append(chosen + 2 * level * RANKS)
        columns.append(2 * (level + 1) * RANKS - 1 - chosen)
    assigned = jnp.stack(columns, axis=1)
    orders = jax.vmap(lambda single: jax.random.permutation(single, N_HEAD))(jax.random.split(order_key, RANKS)).astype(jnp.int32)
    placed = jnp.take_along_axis(assigned, orders, axis=1)
    return jnp.transpose(placed).reshape(BLOCKS).astype(jnp.int32)


def levels(rng, dims, pieces, least, high):
    level = 1.0
    for position, blocks in pieces:
        heights = jax.random.uniform(jax.random.fold_in(jax.random.fold_in(rng, 6), position), (blocks,), jnp.float32, least / len(pieces), high / len(pieces))
        level = level * jnp.repeat(jnp.exp(heights), dims[position] // blocks).reshape((-1,) + (1,) * (len(dims) - 1 - position))
    return level


def normal_values(key, dims, width, limit, cuts=(), kind=jnp.bfloat16):
    entries = jax.random.normal(key, dims, jnp.float32) * width
    if len(cuts) > 0:
        entries = levels(key, dims, cuts, -0.22, 0.18) * entries
    return jnp.clip(entries, min=-limit, max=limit).astype(kind)


def setup_inputs(seed: int = 0) -> dict:
    arg_keys = jax.random.split(jax.random.key(seed), 6)
    return {
        "queries": draw_queries(jax.random.fold_in(arg_keys[5], 71), 0),
        "keys": draw_keys(jax.random.fold_in(arg_keys[5], 71), 0),
        "values": normal_values(arg_keys[2], (TOKENS, KV_HEADS * HEAD_DIM), 1.0, 6.0, ((0, 32),)),
        "grad_out": normal_values(arg_keys[3], (TOKENS, HEADS * HEAD_DIM), 1.0, 6.0, ((0, 32),)),
        "block_order": draw_block_order(jax.random.fold_in(arg_keys[5], 71), 0),
    }


def reference(queries, keys, values, grad_out, block_order):
    group_size = HEADS // KV_HEADS
    score_scale = HEAD_DIM ** -0.5
    row_index = jnp.arange(TOKENS, dtype=jnp.int32)
    positions = jnp.repeat(block_order, TOK_DEV, total_repeat_length=TOKENS) * TOK_DEV + row_index % TOK_DEV
    query_all = queries.reshape(TOKENS, KV_HEADS, group_size, HEAD_DIM)
    grad_all = grad_out.reshape(TOKENS, KV_HEADS, group_size, HEAD_DIM)
    key_all = keys.reshape(TOKENS, KV_HEADS, HEAD_DIM)
    value_all = values.reshape(TOKENS, KV_HEADS, HEAD_DIM)
    block_span = TOK_DEV * 16
    block_count = TOKENS // block_span
    query_parts = []
    key_parts = []
    value_parts = []
    for kv_head in range(KV_HEADS):
        key_head = key_all[:, kv_head].astype(jnp.float32)
        value_head = value_all[:, kv_head].astype(jnp.float32)
        query_head = query_all[:, kv_head]
        grad_head = grad_all[:, kv_head]

        def visit_block(state_in, block_index):
            key_grad, value_grad = state_in
            row_start = (block_index * block_span).astype(jnp.int32)
            query_rows = lax.dynamic_slice_in_dim(query_head, row_start, block_span, 0).astype(jnp.float32)
            grad_rows = lax.dynamic_slice_in_dim(grad_head, row_start, block_span, 0).astype(jnp.float32)
            row_positions = lax.dynamic_slice_in_dim(positions, row_start, block_span, 0)
            scores = jnp.einsum('qgd,kd->gqk', query_rows, key_head) * score_scale
            allowed = row_positions[:, None] >= positions[None, :]
            scores = jnp.where(allowed[None], scores, -jnp.inf)
            row_top = jnp.max(scores, axis=-1, keepdims=True)
            log_total = row_top + jnp.log(jnp.sum(jnp.exp(scores - row_top), axis=-1, keepdims=True))
            probs = jnp.exp(scores - log_total)
            probs_low = lax.optimization_barrier(probs.astype(jnp.bfloat16)).astype(jnp.float32)
            attended = jnp.einsum('gqk,kd->qgd', probs_low, value_head)
            row_dots = jnp.sum(grad_rows * attended, axis=-1)
            prob_grad = jnp.einsum('qgd,kd->gqk', grad_rows, value_head)
            score_grad = probs * (prob_grad - jnp.transpose(row_dots)[:, :, None])
            score_low = lax.optimization_barrier(score_grad.astype(jnp.bfloat16)).astype(jnp.float32)
            query_grad = jnp.einsum('gqk,kd->qgd', score_low, key_head) * score_scale
            key_grad = key_grad + jnp.einsum('gqk,qgd->kd', score_low, query_rows)
            value_grad = value_grad + jnp.einsum('gqk,qgd->kd', probs_low, grad_rows)
            return (key_grad, value_grad), query_grad.astype(jnp.bfloat16)

        empty_grad = jnp.zeros((TOKENS, HEAD_DIM), jnp.float32)
        (key_grad, value_grad), query_grad = lax.scan(visit_block, (empty_grad, empty_grad), jnp.arange(block_count, dtype=jnp.int32))
        query_parts.append(query_grad.reshape(TOKENS, group_size * HEAD_DIM))
        key_parts.append((key_grad * score_scale).astype(jnp.bfloat16))
        value_parts.append(value_grad.astype(jnp.bfloat16))
    return (jnp.concatenate(query_parts, axis=1), jnp.concatenate(key_parts, axis=1), jnp.concatenate(value_parts, axis=1))
```

```python
import functools

import jax
import jax.numpy as jnp
from jax import lax
from jax.experimental import pallas as pl
from jax.experimental.pallas import tpu as pltpu
from jax.sharding import PartitionSpec as P

HEADS = 32
KV_HEADS = 4
HEAD_DIM = 128
GROUP = HEADS // KV_HEADS
SCALE = HEAD_DIM ** (-0.5)
LOG2E = 1.4426950408889634
masked_score = -1e30
VMEM_LIMIT = 60 * 1024 * 1024

NT = (((1,), (1,)), ((), ()))
NN = (((1,), (0,)), ((), ()))


def dot(a, b, dims):
    return lax.dot_general(a, b, dims, preferred_element_type=jnp.float32)


def exchange(array, axis, by):
    length = lax.axis_size(axis)
    return lax.ppermute(array, axis, [(i, i ^ by) for i in range(length)])


def call(body, outs, args, in_spaces, out_space, scratch=()):
    return pl.pallas_call(
        body,
        out_shape=outs,
        in_specs=[pl.BlockSpec(memory_space=s) for s in in_spaces],
        out_specs=[pl.BlockSpec(memory_space=out_space) for _ in outs],
        scratch_shapes=list(scratch),
        compiler_params=pltpu.CompilerParams(vmem_limit_bytes=VMEM_LIMIT),
    )(*args)


def pack_kv(heads, keys_ref, values_ref, *outs):
    me = lax.axis_index("head")
    for i in range(heads):
        columns = pl.ds(pl.multiple_of((me ^ i) * HEAD_DIM, HEAD_DIM), HEAD_DIM)
        outs[i][:, :HEAD_DIM] = keys_ref[:, columns]
        outs[i][:, HEAD_DIM:] = values_ref[:, columns]


def pack_rows(heads, rows_ref, *refs):
    outs, sem = refs[:-1], refs[-1]
    me = lax.axis_index("head")
    width = rows_ref.shape[1] // heads
    copies = []
    for i in range(1, heads):
        columns = pl.ds(pl.multiple_of((me ^ i) * width, width), width)
        copies.append(pltpu.make_async_copy(rows_ref.at[:, columns], outs[i - 1], sem.at[i - 1]))
    for copy in copies:
        copy.start()
    for copy in copies:
        copy.wait()


def join_kv(*refs):
    out = refs[-1]
    me = lax.axis_index("head")
    rows = refs[0].shape[0]
    for i, ref in enumerate(refs[:-1]):
        out[pl.ds(pl.multiple_of((me ^ i) * rows, rows), rows), :] = ref[...]


def main_body(heads, inner, outer, rows_now, order_ref, *refs):
    it = iter(refs)
    q_full = next(it)
    g_full = next(it)
    q_got = [next(it) for _ in range(heads - 1)]
    g_got = [next(it) for _ in range(heads - 1)]
    bundles = [[next(it) for _ in range(inner)] for _ in range(outer)]
    dq_outs = [next(it) for _ in range(heads)]
    same_out = next(it)
    other_outs = [next(it) for _ in range(outer - 1)]
    keys, values, queries, grads, key_t, s_ref, p_ref, dk_ref, dv_ref, dq_ref = it

    block = q_full.shape[0]
    ranks = inner * outer
    chunk = ranks * block
    width = GROUP * HEAD_DIM
    me = lax.axis_index("head")
    z = lax.axis_index("inner")
    o = lax.axis_index("outer")
    rank = z * outer + o

    for e in range(outer):
        for s in range(inner):
            other = (z ^ s) * outer + (o ^ e)
            for a in range(heads):
                at = pl.ds(pl.multiple_of(order_ref[a * ranks + other] * block, block), block)
                keys[at, :] = bundles[e][s][a * block : (a + 1) * block, :HEAD_DIM]
                values[at, :] = bundles[e][s][a * block : (a + 1) * block, HEAD_DIM:]

    place = [order_ref[(me ^ i) * ranks + rank] for i in range(heads)]
    level_of = [p // ranks for p in place]
    for i in range(heads):
        for g in range(GROUP):
            rows = slice(g * block, (g + 1) * block)
            if i == 0:
                cols = pl.ds(pl.multiple_of(me * width + g * HEAD_DIM, HEAD_DIM), HEAD_DIM)
                queries[level_of[0], rows, :] = q_full[:, cols]
                grads[level_of[0], rows, :] = g_full[:, cols]
            else:
                cols = slice(g * HEAD_DIM, (g + 1) * HEAD_DIM)
                queries[level_of[i], rows, :] = q_got[i - 1][:, cols]
                grads[level_of[i], rows, :] = g_got[i - 1][:, cols]

    for c in range(heads):
        key_t[:, c * chunk : (c + 1) * chunk] = keys[c * chunk : (c + 1) * chunk, :].T

    all_rows = GROUP * block
    for level in reversed(range(heads)):
        position = sum(jnp.where(level_of[i] == level, place[i], 0) for i in range(heads))
        shift = position * block - level * chunk
        for r in range(0, all_rows, rows_now):
            q = queries[level, r : r + rows_now, :]
            g = grads[level, r : r + rows_now, :]
            top = None
            for c in range(level + 1):
                span = slice(c * chunk, (c + 1) * chunk)
                s = dot(keys[span, :], q, NT)
                if c == level:
                    u = lax.broadcasted_iota(jnp.int32, s.shape, 0)
                    t = lax.broadcasted_iota(jnp.int32, s.shape, 1) % block
                    s = jnp.where(u <= t + shift, s, masked_score)
                s_ref[span, :] = s
                now = jnp.max(s, axis=0, keepdims=True)
                top = now if top is None else jnp.maximum(top, now)
            total = None
            for c in range(level + 1):
                span = slice(c * chunk, (c + 1) * chunk)
                e = jnp.exp2((s_ref[span, :] - top) * (SCALE * LOG2E))
                s_ref[span, :] = e
                now = jnp.sum(e, axis=0, keepdims=True)
                total = now if total is None else total + now
            inverse = 1.0 / total
            dots = None
            for c in range(level + 1):
                span = slice(c * chunk, (c + 1) * chunk)
                p = s_ref[span, :] * inverse
                s_ref[span, :] = p
                low = p.astype(jnp.bfloat16)
                part = dot(low, g, NN)
                if level == heads - 1 and r == 0:
                    dv_ref[span, :] = part
                else:
                    dv_ref[span, :] += part
                dp = dot(values[span, :], g, NT)
                p_ref[span, :] = dp
                now = jnp.sum(low.astype(jnp.float32) * dp, axis=0, keepdims=True)
                dots = now if dots is None else dots + now
            dq = None
            for c in range(level + 1):
                span = slice(c * chunk, (c + 1) * chunk)
                ds = (s_ref[span, :] * (p_ref[span, :] - dots)).astype(jnp.bfloat16)
                part = dot(ds, q, NN)
                if level == heads - 1 and r == 0:
                    dk_ref[span, :] = part
                else:
                    dk_ref[span, :] += part
                part = dot(key_t[:, span], ds, NN)
                dq = part if dq is None else dq + part
            dq_ref[level, r : r + rows_now, :] = (dq * SCALE).T.astype(jnp.bfloat16)

    for i in range(heads):
        for g in range(GROUP):
            dq_outs[i][:, g * HEAD_DIM : (g + 1) * HEAD_DIM] = dq_ref[
                level_of[i], g * block : (g + 1) * block, :
            ]
    for e in range(outer):
        out = same_out if e == 0 else other_outs[e - 1]
        for s in range(inner):
            other = (z ^ s) * outer + (o ^ e)
            for a in range(heads):
                at = pl.ds(pl.multiple_of(order_ref[a * ranks + other] * block, block), block)
                rows = slice((s * heads + a) * block, (s * heads + a + 1) * block)
                out[rows, :HEAD_DIM] = dk_ref[at, :].astype(out.dtype)
                out[rows, HEAD_DIM:] = dv_ref[at, :].astype(out.dtype)


def sum_cores(parts, *refs):
    ins, outs = refs[:parts], refs[parts:]
    rows = outs[0].shape[0]
    for s, out in enumerate(outs):
        span = slice(s * rows, (s + 1) * rows)
        total = ins[0][span, :].astype(jnp.float32)
        for ref in ins[1:]:
            total = total + ref[span, :].astype(jnp.float32)
        out[...] = total.astype(out.dtype)


def sum_inner(parts, *refs):
    ins, outs = refs[:parts], refs[parts:]
    me = lax.axis_index("head")
    rows = outs[0].shape[0]
    for i, out in enumerate(outs):
        at = pl.ds(pl.multiple_of((me ^ i) * rows, rows), rows)
        total = ins[0][at, :].astype(jnp.float32)
        for ref in ins[1:]:
            total = total + ref[at, :].astype(jnp.float32)
        out[:, :HEAD_DIM] = (total[:, :HEAD_DIM] * SCALE).astype(out.dtype)
        out[:, HEAD_DIM:] = total[:, HEAD_DIM:].astype(out.dtype)


def place_kv(heads, *refs):
    ins, (dk, dv) = refs[:heads], refs[heads:]
    me = lax.axis_index("head")
    for i, ref in enumerate(ins):
        columns = pl.ds(pl.multiple_of((me ^ i) * HEAD_DIM, HEAD_DIM), HEAD_DIM)
        dk[:, columns] = ref[:, :HEAD_DIM]
        dv[:, columns] = ref[:, HEAD_DIM:]


def place_rows(heads, *refs):
    ins, out, sem = refs[:heads], refs[heads], refs[heads + 1]
    me = lax.axis_index("head")
    width = ins[0].shape[1]
    copies = []
    for i in range(heads):
        columns = pl.ds(pl.multiple_of((me ^ i) * width, width), width)
        copies.append(pltpu.make_async_copy(ins[i], out.at[:, columns], sem.at[i]))
    for copy in copies:
        copy.start()
    for copy in copies:
        copy.wait()


def local(queries, keys, values, grad_out, block_order):
    heads = lax.axis_size("head")
    inner = lax.axis_size("inner")
    outer = lax.axis_size("outer")
    block = queries.shape[0]
    ranks = inner * outer
    chunk = ranks * block
    tokens = heads * chunk
    bf16, f32 = jnp.bfloat16, jnp.float32
    V, A, S = pltpu.VMEM, pl.ANY, pltpu.SMEM
    shape = jax.ShapeDtypeStruct
    width = GROUP * HEAD_DIM
    dma = pltpu.SemaphoreType.DMA

    kv_packed = call(
        functools.partial(pack_kv, heads),
        [shape((block, 2 * HEAD_DIM), bf16)] * heads,
        (keys, values), [V] * 2, V,
    )
    kv_got = [kv_packed[0]] + [exchange(kv_packed[i], "head", i) for i in range(1, heads)]
    rows_shape = [shape((block, width), bf16)] * (heads - 1)
    pack = functools.partial(pack_rows, heads)
    q_packed = call(pack, rows_shape, (queries,), [A], A, [dma((heads - 1,))])
    g_packed = call(pack, rows_shape, (grad_out,), [A], A, [dma((heads - 1,))])
    q_got = [exchange(x, "head", i + 1) for i, x in enumerate(q_packed)]
    g_got = [exchange(x, "head", i + 1) for i, x in enumerate(g_packed)]
    mine = call(join_kv, [shape((heads * block, 2 * HEAD_DIM), bf16)], kv_got, [V] * heads, V)[0]
    same = [mine] + [exchange(mine, "inner", s) for s in range(1, inner)]
    bundles = list(same)
    for e in range(1, outer):
        bundles += [exchange(x, "outer", e) for x in same]

    rows_now = GROUP * block if chunk <= 512 else GROUP * block // 2
    results = call(
        functools.partial(main_body, heads, inner, outer, rows_now),
        [shape((block, width), bf16)] * heads
        + [shape((inner * heads * block, 2 * HEAD_DIM), bf16)] * outer,
        (block_order, queries, grad_out, *q_got, *g_got, *bundles),
        [S] + [V] * (2 + 2 * (heads - 1) + inner * outer), V,
        [
            V((tokens, HEAD_DIM), bf16), V((tokens, HEAD_DIM), bf16),
            V((heads, GROUP * block, HEAD_DIM), bf16), V((heads, GROUP * block, HEAD_DIM), bf16),
            V((HEAD_DIM, tokens), bf16),
            V((tokens, rows_now), f32), V((tokens, rows_now), f32),
            V((tokens, HEAD_DIM), f32), V((tokens, HEAD_DIM), f32),
            V((heads, GROUP * block, HEAD_DIM), bf16),
        ],
    )
    dq_parts, same_part, other_parts = results[:heads], results[heads], results[heads + 1 :]
    core_parts = [same_part] + [exchange(x, "outer", e + 1) for e, x in enumerate(other_parts)]
    sums = call(
        functools.partial(sum_cores, outer),
        [shape((heads * block, 2 * HEAD_DIM), bf16)] * inner,
        core_parts, [V] * outer, V,
    )
    inner_parts = [sums[0]] + [exchange(sums[s], "inner", s) for s in range(1, inner)]
    back = call(
        functools.partial(sum_inner, inner),
        [shape((block, 2 * HEAD_DIM), bf16)] * heads,
        inner_parts, [V] * inner, V,
    )
    dq_got = [dq_parts[0]] + [exchange(dq_parts[i], "head", i) for i in range(1, heads)]
    query_back = call(
        functools.partial(place_rows, heads),
        [shape(queries.shape, bf16)], dq_got, [A] * heads, A, [dma((heads,))],
    )[0]
    back_got = [back[0]] + [exchange(back[i], "head", i) for i in range(1, heads)]
    key_back, value_back = call(
        functools.partial(place_kv, heads),
        [shape(keys.shape, bf16)] * 2, back_got, [V] * heads, V,
    )
    return query_back, key_back, value_back


def solution(mesh):
    rows = P(("head", "inner", "outer"), None)
    return jax.shard_map(
        local, mesh=mesh, in_specs=(rows,) * 4 + (P(),), out_specs=(rows,) * 3, check_vma=False
    )
```

```python
import functools

import jax
import jax.numpy as jnp
from jax import lax
from jax.experimental import pallas as pl
from jax.experimental.pallas import tpu as pltpu
from jax.sharding import PartitionSpec as P

HEADS = 32
KV_HEADS = 4
HEAD_DIM = 128
GROUP = HEADS // KV_HEADS
SCALE = HEAD_DIM ** (-0.5)
LOG2E = 1.4426950408889634
masked_score = -1e30

NT = (((1,), (1,)), ((), ()))
NN = (((1,), (0,)), ((), ()))


def dot(a, b, dims):
    return lax.dot_general(a, b, dims, preferred_element_type=jnp.float32)


def exchange(array, axis, by):
    length = lax.axis_size(axis)
    return lax.ppermute(array, axis, [(i, i ^ by) for i in range(length)])


def call(body, outs, args, scratch=(), limit=16):
    arrays, in_specs = [], []
    for array, where in args:
        if where is pltpu.VMEM:
            array = pltpu.with_memory_space_constraint(array, pltpu.VMEM)
        arrays.append(array)
        in_specs.append(pl.BlockSpec(memory_space=pltpu.VMEM if where is None else where))
    shapes, out_specs = [], []
    for dims, dtype, where in outs:
        pinned = where is pltpu.VMEM
        shapes.append(pltpu.VMEM(dims, dtype) if pinned else jax.ShapeDtypeStruct(dims, dtype))
        out_specs.append(pl.BlockSpec(memory_space=pltpu.VMEM if where is None else where))
    return pl.pallas_call(
        body,
        out_shape=shapes,
        in_specs=in_specs,
        out_specs=out_specs,
        scratch_shapes=list(scratch),
        compiler_params=pltpu.CompilerParams(vmem_limit_bytes=limit * 1024 * 1024),
    )(*arrays)


def pack_kv(heads, keys_ref, values_ref, *outs):
    me = lax.axis_index("head")
    for i in range(heads):
        columns = pl.ds(pl.multiple_of((me ^ i) * HEAD_DIM, HEAD_DIM), HEAD_DIM)
        outs[i][:, :HEAD_DIM] = keys_ref[:, columns]
        outs[i][:, HEAD_DIM:] = values_ref[:, columns]


def pack_rows(heads, q_ref, g_ref, *refs):
    outs, sem = refs[:-1], refs[-1]
    me = lax.axis_index("head")
    width = q_ref.shape[1] // heads
    copies = []
    for i in range(heads):
        columns = pl.ds(pl.multiple_of((me ^ i) * width, width), width)
        for j, ref in enumerate((q_ref, g_ref)):
            copies.append(pltpu.make_async_copy(ref.at[:, columns], outs[i].at[j], sem.at[i, j]))
    for copy in copies:
        copy.start()
    for copy in copies:
        copy.wait()


def join_kv(*refs):
    out = refs[-1]
    me = lax.axis_index("head")
    rows = refs[0].shape[0]
    for i, ref in enumerate(refs[:-1]):
        out[pl.ds(pl.multiple_of((me ^ i) * rows, rows), rows), :] = ref[...]


def main_body(heads, inner, outer, rows_now, order_ref, *refs):
    it = iter(refs)
    qg = [next(it) for _ in range(heads)]
    bundles = [[next(it) for _ in range(inner)] for _ in range(outer)]
    dq_outs = [next(it) for _ in range(heads)]
    same_out = next(it)
    other_outs = [next(it) for _ in range(outer - 1)]
    keys, values, queries, grads, key_t, s_ref, p_ref, dk_ref, dv_ref, dq_ref = it

    block = qg[0].shape[1]
    ranks = inner * outer
    chunk = ranks * block
    me = lax.axis_index("head")
    z = lax.axis_index("inner")
    o = lax.axis_index("outer")
    rank = z * outer + o

    for e in range(outer):
        for s in range(inner):
            other = (z ^ s) * outer + (o ^ e)
            for a in range(heads):
                at = pl.ds(pl.multiple_of(order_ref[a * ranks + other] * block, block), block)
                keys[at, :] = bundles[e][s][a * block : (a + 1) * block, :HEAD_DIM]
                values[at, :] = bundles[e][s][a * block : (a + 1) * block, HEAD_DIM:]

    place = [order_ref[(me ^ i) * ranks + rank] for i in range(heads)]
    level_of = [p // ranks for p in place]
    for i in range(heads):
        for g in range(GROUP):
            rows = slice(g * block, (g + 1) * block)
            cols = slice(g * HEAD_DIM, (g + 1) * HEAD_DIM)
            queries[level_of[i], rows, :] = qg[i][0, :, cols]
            grads[level_of[i], rows, :] = qg[i][1, :, cols]

    for c in range(heads):
        key_t[:, c * chunk : (c + 1) * chunk] = keys[c * chunk : (c + 1) * chunk, :].T

    dk_ref[...] = jnp.zeros_like(dk_ref)
    dv_ref[...] = jnp.zeros_like(dv_ref)
    all_rows = GROUP * block
    for level in range(heads):
        position = sum(jnp.where(level_of[i] == level, place[i], 0) for i in range(heads))
        shift = position * block - level * chunk

        def visit(r, level=level, shift=shift):
            here = pl.ds(pl.multiple_of(r * rows_now, rows_now), rows_now)
            q = queries[level, here, :]
            g = grads[level, here, :]
            top = None
            for c in range(level + 1):
                span = slice(c * chunk, (c + 1) * chunk)
                s = dot(keys[span, :], q, NT)
                if c == level:
                    u = lax.broadcasted_iota(jnp.int32, s.shape, 0)
                    t = lax.broadcasted_iota(jnp.int32, s.shape, 1) % block
                    s = jnp.where(u <= t + shift, s, masked_score)
                s_ref[span, :] = s
                now = jnp.max(s, axis=0, keepdims=True)
                top = now if top is None else jnp.maximum(top, now)
            total, dots = None, None
            for c in range(level + 1):
                span = slice(c * chunk, (c + 1) * chunk)
                e = jnp.exp2((s_ref[span, :] - top) * (SCALE * LOG2E))
                s_ref[span, :] = e
                now = jnp.sum(e, axis=0, keepdims=True)
                total = now if total is None else total + now
                dp = dot(values[span, :], g, NT)
                p_ref[span, :] = dp
                now = jnp.sum(e * dp, axis=0, keepdims=True)
                dots = now if dots is None else dots + now
            inverse = 1.0 / total
            dots = dots * inverse
            dq = None
            for c in range(level + 1):
                span = slice(c * chunk, (c + 1) * chunk)
                p = s_ref[span, :] * inverse
                dv_ref[span, :] += dot(p.astype(jnp.bfloat16), g, NN)
                ds = (p * (p_ref[span, :] - dots)).astype(jnp.bfloat16)
                dk_ref[span, :] += dot(ds, q, NN)
                part = dot(key_t[:, span], ds, NN)
                dq = part if dq is None else dq + part
            dq_ref[level, here, :] = (dq * SCALE).T.astype(jnp.bfloat16)

        if all_rows == rows_now:
            visit(0)
        else:
            pl.loop(0, all_rows // rows_now)(visit)

    for i in range(heads):
        for g in range(GROUP):
            dq_outs[i][:, g * HEAD_DIM : (g + 1) * HEAD_DIM] = dq_ref[
                level_of[i], g * block : (g + 1) * block, :
            ]
    for e in range(outer):
        out = same_out if e == 0 else other_outs[e - 1]
        for s in range(inner):
            other = (z ^ s) * outer + (o ^ e)
            for a in range(heads):
                at = pl.ds(pl.multiple_of(order_ref[a * ranks + other] * block, block), block)
                rows = slice((s * heads + a) * block, (s * heads + a + 1) * block)
                out[rows, :HEAD_DIM] = dk_ref[at, :].astype(out.dtype)
                out[rows, HEAD_DIM:] = dv_ref[at, :].astype(out.dtype)


def attend(qg, bundles, block_order, rows_now):
    heads, inner, outer = (lax.axis_size(n) for n in ("head", "inner", "outer"))
    block = qg[0].shape[1]
    tokens = heads * inner * outer * block
    rows = GROUP * block
    bf16, f32, V = jnp.bfloat16, jnp.float32, pltpu.VMEM
    return call(
        functools.partial(main_body, heads, inner, outer, rows_now),
        [((block, GROUP * HEAD_DIM), bf16, V)] * heads
        + [((inner * heads * block, 2 * HEAD_DIM), bf16, V)] * outer,
        [(block_order, pltpu.SMEM)] + [(x, V) for x in qg + bundles],
        [
            V((tokens, HEAD_DIM), bf16), V((tokens, HEAD_DIM), bf16),
            V((heads, rows, HEAD_DIM), bf16), V((heads, rows, HEAD_DIM), bf16),
            V((HEAD_DIM, tokens), bf16),
            V((tokens, rows_now), f32), V((tokens, rows_now), f32),
            V((tokens, HEAD_DIM), f32), V((tokens, HEAD_DIM), f32),
            V((heads, rows, HEAD_DIM), bf16),
        ],
        limit=24 if tokens <= 2048 else 44,
    )


def sum_cores(parts, *refs):
    ins, outs = refs[:parts], refs[parts:]
    rows = outs[0].shape[0]
    for s, out in enumerate(outs):
        span = slice(s * rows, (s + 1) * rows)
        total = ins[0][span, :].astype(jnp.float32)
        for ref in ins[1:]:
            total = total + ref[span, :].astype(jnp.float32)
        out[...] = total.astype(out.dtype)


def sum_inner(parts, *refs):
    ins, outs = refs[:parts], refs[parts:]
    me = lax.axis_index("head")
    rows = outs[0].shape[0]
    for i, out in enumerate(outs):
        at = pl.ds(pl.multiple_of((me ^ i) * rows, rows), rows)
        total = ins[0][at, :].astype(jnp.float32)
        for ref in ins[1:]:
            total = total + ref[at, :].astype(jnp.float32)
        out[:, :HEAD_DIM] = (total[:, :HEAD_DIM] * SCALE).astype(out.dtype)
        out[:, HEAD_DIM:] = total[:, HEAD_DIM:].astype(out.dtype)


def place_kv(heads, *refs):
    ins, (dk, dv) = refs[:heads], refs[heads:]
    me = lax.axis_index("head")
    for i, ref in enumerate(ins):
        columns = pl.ds(pl.multiple_of((me ^ i) * HEAD_DIM, HEAD_DIM), HEAD_DIM)
        dk[:, columns] = ref[:, :HEAD_DIM]
        dv[:, columns] = ref[:, HEAD_DIM:]


def place_rows(heads, *refs):
    ins, out, sem = refs[:heads], refs[heads], refs[heads + 1]
    me = lax.axis_index("head")
    width = ins[0].shape[1]
    copies = []
    for i in range(heads):
        columns = pl.ds(pl.multiple_of((me ^ i) * width, width), width)
        copies.append(pltpu.make_async_copy(ins[i], out.at[:, columns], sem.at[i]))
    for copy in copies:
        copy.start()
    for copy in copies:
        copy.wait()


def local(queries, keys, values, grad_out, block_order):
    heads, inner, outer = (lax.axis_size(n) for n in ("head", "inner", "outer"))
    block = queries.shape[0]
    chunk = inner * outer * block
    bf16 = jnp.bfloat16
    V, A = pltpu.VMEM, pl.ANY
    width = GROUP * HEAD_DIM
    dma = pltpu.SemaphoreType.DMA
    pair = 2 * HEAD_DIM

    kv_packed = call(
        functools.partial(pack_kv, heads),
        [((block, pair), bf16, V)] * heads,
        [(keys, None), (values, None)],
    )
    kv_packed, queries, grad_out = lax.optimization_barrier((kv_packed, queries, grad_out))
    kv_got = [kv_packed[0]] + [exchange(kv_packed[i], "head", i) for i in range(1, heads)]
    qg_packed = call(
        functools.partial(pack_rows, heads),
        [((2, block, width), bf16, V)] * heads,
        [(queries, A), (grad_out, A)],
        [dma((heads, 2))],
    )
    qg = [qg_packed[0]] + [exchange(qg_packed[i], "head", i) for i in range(1, heads)]
    mine = call(
        functools.partial(join_kv), [((heads * block, pair), bf16, V)], [(x, V) for x in kv_got]
    )[0]
    same = [mine] + [exchange(mine, "inner", s) for s in range(1, inner)]
    bundles = list(same)
    for e in range(1, outer):
        bundles += [exchange(x, "outer", e) for x in same]

    rows_now = GROUP * block if chunk <= 512 else GROUP * block // 2
    results = attend(qg, bundles, block_order, rows_now)
    dq_parts, same_part, other_parts = results[:heads], results[heads], results[heads + 1 :]
    core_parts = [same_part] + [exchange(x, "outer", e + 1) for e, x in enumerate(other_parts)]
    sums = call(
        functools.partial(sum_cores, outer),
        [((heads * block, pair), bf16, V)] * inner,
        [(x, V) for x in core_parts],
    )
    inner_parts = [sums[0]] + [exchange(sums[s], "inner", s) for s in range(1, inner)]
    dq_got = [dq_parts[0]] + [exchange(dq_parts[i], "head", i) for i in range(1, heads)]
    back = call(
        functools.partial(sum_inner, inner),
        [((block, pair), bf16, V)] * heads,
        [(x, V) for x in inner_parts],
    )
    back_got = [back[0]] + [exchange(back[i], "head", i) for i in range(1, heads)]
    query_back = call(
        functools.partial(place_rows, heads),
        [(queries.shape, bf16, A)], [(x, V) for x in dq_got], [dma((heads,))],
    )[0]
    key_back, value_back = call(
        functools.partial(place_kv, heads),
        [(keys.shape, bf16, None)] * 2, [(x, V) for x in back_got],
    )
    return query_back, key_back, value_back


def solution(mesh):
    rows = P(("head", "inner", "outer"), None)
    return jax.shard_map(
        local, mesh=mesh, in_specs=(rows,) * 4 + (P(),), out_specs=(rows,) * 3, check_vma=False
    )
```

```python
import functools

import jax
import jax.numpy as jnp
from jax import lax
from jax.experimental import pallas as pl
from jax.experimental.pallas import tpu as pltpu
from jax.sharding import PartitionSpec as P

HEADS = 32
KV_HEADS = 4
HEAD_DIM = 128
GROUP = HEADS // KV_HEADS
SCALE = HEAD_DIM ** (-0.5)
LOG2E = 1.4426950408889634
masked_score = -1e30

NT = (((1,), (1,)), ((), ()))
NN = (((1,), (0,)), ((), ()))


def dot(a, b, dims):
    return lax.dot_general(a, b, dims, preferred_element_type=jnp.float32)


def exchange(array, axis, by):
    length = lax.axis_size(axis)
    return lax.ppermute(array, axis, [(i, i ^ by) for i in range(length)])


def trade(pieces, axis, order=None):
    got = list(pieces)
    for i in order or range(1, len(pieces)):
        got[i] = exchange(pieces[i], axis, i)
    return got


def call(body, outs, args, scratch=(), limit=16):
    arrays, in_specs = [], []
    for array, where in args:
        if where in (pltpu.VMEM, pltpu.HBM):
            array = pltpu.with_memory_space_constraint(array, where)
        arrays.append(array)
        in_specs.append(pl.BlockSpec(memory_space=pltpu.VMEM if where is None else where))
    shapes, out_specs = [], []
    for dims, dtype, where in outs:
        pinned = where is pltpu.VMEM
        shapes.append(pltpu.VMEM(dims, dtype) if pinned else jax.ShapeDtypeStruct(dims, dtype))
        out_specs.append(pl.BlockSpec(memory_space=pltpu.VMEM if where is None else where))
    return pl.pallas_call(
        body,
        out_shape=shapes,
        in_specs=in_specs,
        out_specs=out_specs,
        scratch_shapes=list(scratch),
        compiler_params=pltpu.CompilerParams(vmem_limit_bytes=limit * 1024 * 1024),
    )(*arrays)


def pack(heads, *refs):
    ins, outs, sem = refs[:2], refs[2:-1], refs[-1]
    me = lax.axis_index("head")
    width = ins[0].shape[1] // heads
    copies = []
    for i, out in enumerate(outs):
        columns = pl.ds(pl.multiple_of((me ^ i) * width, width), width)
        for j, ref in enumerate(ins):
            part = out.at[j] if len(out.shape) == 3 else out.at[:, j * width : (j + 1) * width]
            copies.append(pltpu.make_async_copy(ref.at[:, columns], part, sem.at[i, j]))
    for copy in copies:
        copy.start()
    for copy in copies:
        copy.wait()


def join_kv(*refs):
    out = refs[-1]
    me = lax.axis_index("head")
    rows = refs[0].shape[0]
    for i, ref in enumerate(refs[:-1]):
        out[pl.ds(pl.multiple_of((me ^ i) * rows, rows), rows), :] = ref[...]


def main_body(heads, inner, outer, rows_now, order_ref, *refs):
    it = iter(refs)
    qg = [next(it) for _ in range(heads)]
    bundles = [[next(it) for _ in range(inner)] for _ in range(outer)]
    dq_outs = [next(it) for _ in range(heads)]
    same_out = next(it)
    other_outs = [next(it) for _ in range(outer - 1)]
    keys, values, queries, grads, key_t, s_ref, p_ref, dk_ref, dv_ref, dq_ref = it

    block = qg[0].shape[1]
    ranks = inner * outer
    chunk = ranks * block
    me = lax.axis_index("head")
    z = lax.axis_index("inner")
    o = lax.axis_index("outer")
    rank = z * outer + o

    for e in range(outer):
        for s in range(inner):
            other = (z ^ s) * outer + (o ^ e)
            for a in range(heads):
                at = pl.ds(pl.multiple_of(order_ref[a * ranks + other] * block, block), block)
                keys[at, :] = bundles[e][s][a * block : (a + 1) * block, :HEAD_DIM]
                values[at, :] = bundles[e][s][a * block : (a + 1) * block, HEAD_DIM:]

    place = [order_ref[(me ^ i) * ranks + rank] for i in range(heads)]
    level_of = [p // ranks for p in place]
    for i in range(heads):
        for g in range(GROUP):
            rows = slice(g * block, (g + 1) * block)
            cols = slice(g * HEAD_DIM, (g + 1) * HEAD_DIM)
            queries[level_of[i], rows, :] = qg[i][0, :, cols]
            grads[level_of[i], rows, :] = qg[i][1, :, cols]

    for c in range(heads):
        key_t[:, c * chunk : (c + 1) * chunk] = keys[c * chunk : (c + 1) * chunk, :].T

    dk_ref[...] = jnp.zeros_like(dk_ref)
    dv_ref[...] = jnp.zeros_like(dv_ref)
    all_rows = GROUP * block
    for level in range(heads):
        position = sum(jnp.where(level_of[i] == level, place[i], 0) for i in range(heads))
        shift = position * block - level * chunk

        def visit(r, level=level, shift=shift):
            here = pl.ds(pl.multiple_of(r * rows_now, rows_now), rows_now)
            q = queries[level, here, :]
            g = grads[level, here, :]
            g_t = g.T
            top = None
            for c in range(level + 1):
                span = slice(c * chunk, (c + 1) * chunk)
                s = dot(keys[span, :], q, NT)
                if c == level:
                    u = lax.broadcasted_iota(jnp.int32, s.shape, 0)
                    t = lax.broadcasted_iota(jnp.int32, s.shape, 1) % block
                    s = jnp.where(u <= t + shift, s, masked_score)
                s_ref[span, :] = s
                now = jnp.max(s, axis=0, keepdims=True)
                top = now if top is None else jnp.maximum(top, now)
            total, dots = None, None
            for c in range(level + 1):
                span = slice(c * chunk, (c + 1) * chunk)
                e = jnp.exp2((s_ref[span, :] - top) * (SCALE * LOG2E))
                s_ref[span, :] = e
                now = jnp.sum(e, axis=0, keepdims=True)
                total = now if total is None else total + now
                dp = dot(values[span, :], g, NT)
                p_ref[span, :] = dp
                now = jnp.sum(e * dp, axis=0, keepdims=True)
                dots = now if dots is None else dots + now
            inverse = 1.0 / total
            dots = dots * inverse
            dq = None
            for c in range(level + 1):
                span = slice(c * chunk, (c + 1) * chunk)
                p = s_ref[span, :] * inverse
                dv_ref[span, :] += dot(g_t, p.astype(jnp.bfloat16), NT).T
                ds = (p * (p_ref[span, :] - dots)).astype(jnp.bfloat16)
                dk_ref[span, :] += dot(ds, q, NN)
                part = dot(key_t[:, span], ds, NN)
                dq = part if dq is None else dq + part
            dq_ref[level, here, :] = (dq * SCALE).T.astype(jnp.bfloat16)

        if all_rows == rows_now:
            visit(0)
        else:
            pl.loop(0, all_rows // rows_now)(visit)

    for i in range(heads):
        for g in range(GROUP):
            dq_outs[i][:, g * HEAD_DIM : (g + 1) * HEAD_DIM] = dq_ref[
                level_of[i], g * block : (g + 1) * block, :
            ]
    for e in range(outer):
        out = same_out if e == 0 else other_outs[e - 1]
        for s in range(inner):
            other = (z ^ s) * outer + (o ^ e)
            for a in range(heads):
                at = pl.ds(pl.multiple_of(order_ref[a * ranks + other] * block, block), block)
                rows = slice((s * heads + a) * block, (s * heads + a + 1) * block)
                out[rows, :HEAD_DIM] = dk_ref[at, :].astype(out.dtype)
                out[rows, HEAD_DIM:] = dv_ref[at, :].astype(out.dtype)


def attend(qg, bundles, block_order, rows_now):
    heads, inner, outer = (lax.axis_size(n) for n in ("head", "inner", "outer"))
    block = qg[0].shape[1]
    tokens = heads * inner * outer * block
    rows = GROUP * block
    bf16, f32, V = jnp.bfloat16, jnp.float32, pltpu.VMEM
    return call(
        functools.partial(main_body, heads, inner, outer, rows_now),
        [((block, GROUP * HEAD_DIM), bf16, V)] * heads
        + [((inner * heads * block, 2 * HEAD_DIM), bf16, V)] * outer,
        [(block_order, pltpu.SMEM)] + [(x, V) for x in qg + bundles],
        [
            V((tokens, HEAD_DIM), bf16), V((tokens, HEAD_DIM), bf16),
            V((heads, rows, HEAD_DIM), bf16), V((heads, rows, HEAD_DIM), bf16),
            V((HEAD_DIM, tokens), bf16),
            V((tokens, rows_now), f32), V((tokens, rows_now), f32),
            V((tokens, HEAD_DIM), f32), V((tokens, HEAD_DIM), f32),
            V((heads, rows, HEAD_DIM), bf16),
        ],
        limit=24 if tokens <= 2048 else 44,
    )


def sum_cores(parts, *refs):
    ins, outs = refs[:parts], refs[parts:]
    rows = outs[0].shape[0]
    for s, out in enumerate(outs):
        span = slice(s * rows, (s + 1) * rows)
        total = ins[0][span, :].astype(jnp.float32)
        for ref in ins[1:]:
            total = total + ref[span, :].astype(jnp.float32)
        out[...] = total.astype(out.dtype)


def sum_inner(parts, *refs):
    ins, outs = refs[:parts], refs[parts:]
    me = lax.axis_index("head")
    rows = outs[0].shape[0]
    for i, out in enumerate(outs):
        at = pl.ds(pl.multiple_of((me ^ i) * rows, rows), rows)
        total = ins[0][at, :].astype(jnp.float32)
        for ref in ins[1:]:
            total = total + ref[at, :].astype(jnp.float32)
        out[:, :HEAD_DIM] = (total[:, :HEAD_DIM] * SCALE).astype(out.dtype)
        out[:, HEAD_DIM:] = total[:, HEAD_DIM:].astype(out.dtype)


def place_kv(heads, *refs):
    ins, (dk, dv) = refs[:heads], refs[heads:]
    me = lax.axis_index("head")
    for i, ref in enumerate(ins):
        columns = pl.ds(pl.multiple_of((me ^ i) * HEAD_DIM, HEAD_DIM), HEAD_DIM)
        dk[:, columns] = ref[:, :HEAD_DIM]
        dv[:, columns] = ref[:, HEAD_DIM:]


def place_rows(heads, *refs):
    ins, out, sem = refs[:heads], refs[heads], refs[heads + 1]
    me = lax.axis_index("head")
    width = ins[0].shape[1]
    copies = []
    for i in range(heads):
        columns = pl.ds(pl.multiple_of((me ^ i) * width, width), width)
        copies.append(pltpu.make_async_copy(ins[i], out.at[:, columns], sem.at[i]))
    for copy in copies:
        copy.start()
    for copy in copies:
        copy.wait()


def local(queries, keys, values, grad_out, block_order):
    heads, inner, outer = (lax.axis_size(n) for n in ("head", "inner", "outer"))
    block = queries.shape[0]
    chunk = inner * outer * block
    bf16 = jnp.bfloat16
    V, A = pltpu.VMEM, pl.ANY
    width = GROUP * HEAD_DIM
    dma = pltpu.SemaphoreType.DMA
    pair = 2 * HEAD_DIM

    H = pltpu.HBM
    kv_packed = call(
        functools.partial(pack, heads),
        [((block, pair), bf16, V)] * heads, [(keys, H), (values, H)], [dma((heads, 2))],
    )
    kv_packed, queries, grad_out = lax.optimization_barrier((kv_packed, queries, grad_out))
    qg_packed = call(
        functools.partial(pack, heads),
        [((2, block, width), bf16, V)] * heads, [(queries, H), (grad_out, H)], [dma((heads, 2))],
    )
    far_first = list(reversed(range(1, heads)))
    kv_got = trade(kv_packed, "head", far_first)
    kv_got, qg_packed = lax.optimization_barrier((kv_got, qg_packed))
    qg = [qg_packed[0]] + [exchange(qg_packed[i], "head", i) for i in range(1, heads - 1)]
    last, qg = lax.optimization_barrier((qg_packed[-1], qg))
    qg.append(exchange(last, "head", heads - 1))
    mine = call(
        functools.partial(join_kv), [((heads * block, pair), bf16, V)], [(x, V) for x in kv_got]
    )[0]
    same = [mine] + [exchange(mine, "inner", s) for s in range(1, inner)]
    bundles = list(same)
    early, _ = lax.optimization_barrier((mine, qg[1:-1]))
    for e in range(1, outer):
        bundles += [exchange(x, "outer", e) for x in [early] + same[1:]]

    rows_now = GROUP * block if chunk <= 512 else GROUP * block // 2
    results = attend(qg, bundles, block_order, rows_now)
    dq_parts, same_part, other_parts = results[:heads], results[heads], results[heads + 1 :]
    core_parts = [same_part] + [exchange(x, "outer", e + 1) for e, x in enumerate(other_parts)]
    sums = call(
        functools.partial(sum_cores, outer),
        [((heads * block, pair), bf16, V)] * inner,
        [(x, V) for x in core_parts],
    )
    inner_parts = [sums[0]] + [exchange(sums[s], "inner", s) for s in range(1, inner)]
    dq_got = [dq_parts[0]] + [exchange(dq_parts[i], "head", i) for i in range(1, heads)]
    back = call(
        functools.partial(sum_inner, inner),
        [((block, pair), bf16, V)] * heads,
        [(x, V) for x in inner_parts],
    )
    back_got = trade(back, "head", far_first)
    query_back = call(
        functools.partial(place_rows, heads),
        [(queries.shape, bf16, A)], [(x, V) for x in dq_got], [dma((heads,))],
    )[0]
    key_back, value_back = call(
        functools.partial(place_kv, heads),
        [(keys.shape, bf16, None)] * 2, [(x, V) for x in back_got],
    )
    return query_back, key_back, value_back


def solution(mesh):
    rows = P(("head", "inner", "outer"), None)
    return jax.shard_map(
        local, mesh=mesh, in_specs=(rows,) * 4 + (P(),), out_specs=(rows,) * 3, check_vma=False
    )
```

```python
import functools

import jax
import jax.numpy as jnp
from jax import lax
from jax.experimental import pallas as pl
from jax.experimental.pallas import tpu as pltpu
from jax.sharding import PartitionSpec as P

HEADS = 32
KV_HEADS = 4
HEAD_DIM = 128
GROUP = HEADS // KV_HEADS
SCALE = HEAD_DIM ** (-0.5)
LOG2E = 1.4426950408889634
masked_score = -1e30

NT = (((1,), (1,)), ((), ()))
NN = (((1,), (0,)), ((), ()))


def dot(a, b, dims):
    return lax.dot_general(a, b, dims, preferred_element_type=jnp.float32)


def exchange(array, axis, by):
    length = lax.axis_size(axis)
    return lax.ppermute(array, axis, [(i, i ^ by) for i in range(length)])


def trade(pieces, axis, order=None):
    got = list(pieces)
    for i in order or range(1, len(pieces)):
        got[i] = exchange(pieces[i], axis, i)
    return got


def call(body, outs, args, scratch=(), limit=16):
    arrays, in_specs = [], []
    for array, where in args:
        if where in (pltpu.VMEM, pltpu.HBM):
            array = pltpu.with_memory_space_constraint(array, where)
        arrays.append(array)
        in_specs.append(pl.BlockSpec(memory_space=pltpu.VMEM if where is None else where))
    shapes, out_specs = [], []
    for dims, dtype, where in outs:
        pinned = where is pltpu.VMEM
        shapes.append(pltpu.VMEM(dims, dtype) if pinned else jax.ShapeDtypeStruct(dims, dtype))
        out_specs.append(pl.BlockSpec(memory_space=pltpu.VMEM if where is None else where))
    return pl.pallas_call(
        body,
        out_shape=shapes,
        in_specs=in_specs,
        out_specs=out_specs,
        scratch_shapes=list(scratch),
        compiler_params=pltpu.CompilerParams(vmem_limit_bytes=limit * 1024 * 1024),
    )(*arrays)


def pack(heads, count, *refs):
    ins, outs, sem = refs[:count], refs[count:-1], refs[-1]
    me = lax.axis_index("head")
    width = ins[0].shape[1] // heads
    copies = []
    for i, out in enumerate(outs[:heads]):
        columns = pl.ds(pl.multiple_of((me ^ i) * width, width), width)
        for j, ref in enumerate(ins[:2]):
            part = out.at[j] if len(out.shape) == 3 else out.at[:, j * width : (j + 1) * width]
            copies.append(pltpu.make_async_copy(ref.at[:, columns], part, sem.at[i, j]))
    for n, (ref, out) in enumerate(zip(ins[2:], outs[heads:])):
        copies.append(pltpu.make_async_copy(ref, out, sem.at[heads + n, 0]))
    for copy in copies:
        copy.start()
    for copy in copies:
        copy.wait()


def join_kv(*refs):
    out = refs[-1]
    me = lax.axis_index("head")
    rows = refs[0].shape[0]
    for i, ref in enumerate(refs[:-1]):
        out[pl.ds(pl.multiple_of((me ^ i) * rows, rows), rows), :] = ref[...]


def main_body(heads, inner, outer, rows_now, late, order_ref, *refs):
    it = iter(refs)
    qg = [next(it) for _ in range(heads)]
    bundles = [[next(it) for _ in range(inner)] for _ in range(outer)]
    same_out = next(it)
    other_outs = [next(it) for _ in range(outer - 1)]
    if late:
        ds_out, keys, level_ref = next(it), next(it), next(it)
        values, queries, grads, s_ref, p_ref, dk_ref, dv_ref = it
    else:
        ds_out, dq_outs = None, [next(it) for _ in range(heads)]
        values, queries, grads, s_ref, p_ref, dk_ref, dv_ref, keys, key_t, dq_ref = it

    block = qg[0].shape[1]
    ranks = inner * outer
    chunk = ranks * block
    me = lax.axis_index("head")
    z = lax.axis_index("inner")
    o = lax.axis_index("outer")
    rank = z * outer + o

    for e in range(outer):
        for s in range(inner):
            other = (z ^ s) * outer + (o ^ e)
            for a in range(heads):
                at = pl.ds(pl.multiple_of(order_ref[a * ranks + other] * block, block), block)
                keys[at, :] = bundles[e][s][a * block : (a + 1) * block, :HEAD_DIM]
                values[at, :] = bundles[e][s][a * block : (a + 1) * block, HEAD_DIM:]

    place = [order_ref[(me ^ i) * ranks + rank] for i in range(heads)]
    level_of = [p // ranks for p in place]
    for i in range(heads):
        for g in range(GROUP):
            rows = slice(g * block, (g + 1) * block)
            cols = slice(g * HEAD_DIM, (g + 1) * HEAD_DIM)
            queries[level_of[i], rows, :] = qg[i][0, :, cols]
            grads[level_of[i], rows, :] = qg[i][1, :, cols]

    if not late:
        for c in range(heads):
            key_t[:, c * chunk : (c + 1) * chunk] = keys[c * chunk : (c + 1) * chunk, :].T

    all_rows = GROUP * block
    if rows_now < all_rows:
        dk_ref[...] = jnp.zeros_like(dk_ref)
        dv_ref[...] = jnp.zeros_like(dv_ref)
    for level in reversed(range(heads)):
        position = sum(jnp.where(level_of[i] == level, place[i], 0) for i in range(heads))
        shift = position * block - level * chunk

        def visit(r, level=level, shift=shift):
            here = pl.ds(pl.multiple_of(r * rows_now, rows_now), rows_now)
            q = queries[level, here, :]
            g = grads[level, here, :]
            g_t = g.T
            top = None
            for c in range(level + 1):
                span = slice(c * chunk, (c + 1) * chunk)
                s = dot(keys[span, :], q, NT)
                if c == level:
                    u = lax.broadcasted_iota(jnp.int32, s.shape, 0)
                    t = lax.broadcasted_iota(jnp.int32, s.shape, 1) % block
                    s = jnp.where(u <= t + shift, s, masked_score)
                s_ref[span, :] = s
                now = jnp.max(s, axis=0, keepdims=True)
                top = now if top is None else jnp.maximum(top, now)
            total, dots = None, None
            for c in range(level + 1):
                span = slice(c * chunk, (c + 1) * chunk)
                e = jnp.exp2((s_ref[span, :] - top) * (SCALE * LOG2E))
                s_ref[span, :] = e
                now = jnp.sum(e, axis=0, keepdims=True)
                total = now if total is None else total + now
                dp = dot(values[span, :], g, NT)
                p_ref[span, :] = dp
                now = jnp.sum(e * dp, axis=0, keepdims=True)
                dots = now if dots is None else dots + now
            inverse = 1.0 / total
            dots = dots * inverse
            dq = None
            for c in range(level + 1):
                span = slice(c * chunk, (c + 1) * chunk)
                p = s_ref[span, :] * inverse
                first = level == heads - 1 and rows_now == all_rows
                part = dot(g_t, p.astype(jnp.bfloat16), NT).T
                dv_ref[span, :] = part if first else dv_ref[span, :] + part
                ds = (p * (p_ref[span, :] - dots)).astype(jnp.bfloat16)
                part = dot(ds, q, NN)
                dk_ref[span, :] = part if first else dk_ref[span, :] + part
                if ds_out is not None:
                    ds_out[level * (level + 1) // 2 + c] = ds
                    continue
                part = dot(key_t[:, span], ds, NN)
                dq = part if dq is None else dq + part
            if ds_out is None:
                dq_ref[level, here, :] = (dq * SCALE).T.astype(jnp.bfloat16)

        if all_rows == rows_now:
            visit(0)
        else:
            pl.loop(0, all_rows // rows_now)(visit)

    if late:
        for i in range(heads):
            level_ref[i] = jnp.full(level_ref.shape[1:], level_of[i], jnp.int32)
    else:
        hand_out(dq_outs, dq_ref, level_of)
    for e in range(outer):
        out = same_out if e == 0 else other_outs[e - 1]
        for s in range(inner):
            other = (z ^ s) * outer + (o ^ e)
            for a in range(heads):
                at = pl.ds(pl.multiple_of(order_ref[a * ranks + other] * block, block), block)
                rows = slice((s * heads + a) * block, (s * heads + a + 1) * block)
                out[rows, :HEAD_DIM] = dk_ref[at, :].astype(out.dtype)
                out[rows, HEAD_DIM:] = dv_ref[at, :].astype(out.dtype)


def hand_out(dq_outs, dq_ref, level_of):
    block = dq_outs[0].shape[0]
    for out, level in zip(dq_outs, level_of):
        for g in range(GROUP):
            out[:, g * HEAD_DIM : (g + 1) * HEAD_DIM] = dq_ref[level, g * block : (g + 1) * block, :]


def query_body(heads, ds_ref, keys, level_ref, *dq_outs):
    chunk = ds_ref.shape[1]
    block = dq_outs[0].shape[0]
    by_level = []
    key_t = [keys[c * chunk : (c + 1) * chunk, :].T for c in range(heads)]
    for level in range(heads):
        dq = None
        for c in range(level + 1):
            ds = ds_ref[level * (level + 1) // 2 + c]
            part = dot(key_t[c], ds, NN)
            dq = part if dq is None else dq + part
        by_level.append((dq * SCALE).T)
    for i, out in enumerate(dq_outs):
        for g in range(GROUP):
            rows = slice(g * block, (g + 1) * block)
            piece = by_level[0][rows, :]
            for level in range(1, heads):
                piece = jnp.where(level_ref[i] == level, by_level[level][rows, :], piece)
            out[:, g * HEAD_DIM : (g + 1) * HEAD_DIM] = piece.astype(out.dtype)


def attend(qg, bundles, block_order, rows_now):
    heads, inner, outer = (lax.axis_size(n) for n in ("head", "inner", "outer"))
    block = qg[0].shape[1]
    chunk = inner * outer * block
    tokens = heads * chunk
    rows = GROUP * block
    steps = heads * (heads + 1) // 2
    bf16, f32, V = jnp.bfloat16, jnp.float32, pltpu.VMEM
    late = rows_now == rows
    dq_outs = [((block, GROUP * HEAD_DIM), bf16, V)] * heads
    outs = [((inner * heads * block, 2 * HEAD_DIM), bf16, V)] * outer
    kept = [
        ((steps, chunk, rows), bf16, V), ((tokens, HEAD_DIM), bf16, V), ((heads, block, HEAD_DIM), jnp.int32, V)
    ]
    scratch = [
        V((tokens, HEAD_DIM), bf16),
        V((heads, rows, HEAD_DIM), bf16), V((heads, rows, HEAD_DIM), bf16),
        V((tokens, rows_now), f32), V((tokens, rows_now), f32),
        V((tokens, HEAD_DIM), f32), V((tokens, HEAD_DIM), f32),
    ]
    results = call(
        functools.partial(main_body, heads, inner, outer, rows_now, late),
        outs + (kept if late else dq_outs),
        [(block_order, pltpu.SMEM)] + [(x, V) for x in qg + bundles],
        scratch + ([] if late else [
            V((tokens, HEAD_DIM), bf16), V((HEAD_DIM, tokens), bf16), V((heads, rows, HEAD_DIM), bf16)
        ]),
        limit=24 if tokens <= 2048 else 44,
    )
    if not late:
        return results[:outer], lambda *after: results[outer:]

    def query_grads(*after):
        (ds, *others), _ = lax.optimization_barrier((results[outer:], after))
        return call(
            functools.partial(query_body, heads), dq_outs, [(x, V) for x in (ds, *others)]
        )

    return results[:outer], query_grads


def sum_cores(parts, *refs):
    ins, outs = refs[:parts], refs[parts:]
    rows = outs[0].shape[0]
    for s, out in enumerate(outs):
        span = slice(s * rows, (s + 1) * rows)
        total = ins[0][span, :].astype(jnp.float32)
        for ref in ins[1:]:
            total = total + ref[span, :].astype(jnp.float32)
        out[...] = total.astype(out.dtype)


def sum_inner(parts, *refs):
    ins, outs = refs[:parts], refs[parts:]
    me = lax.axis_index("head")
    rows = outs[0].shape[0]
    for i, out in enumerate(outs):
        at = pl.ds(pl.multiple_of((me ^ i) * rows, rows), rows)
        total = ins[0][at, :].astype(jnp.float32)
        for ref in ins[1:]:
            total = total + ref[at, :].astype(jnp.float32)
        out[:, :HEAD_DIM] = (total[:, :HEAD_DIM] * SCALE).astype(out.dtype)
        out[:, HEAD_DIM:] = total[:, HEAD_DIM:].astype(out.dtype)


def place_kv(heads, *refs):
    ins, (dk, dv) = refs[:heads], refs[heads:]
    me = lax.axis_index("head")
    for i, ref in enumerate(ins):
        columns = pl.ds(pl.multiple_of((me ^ i) * HEAD_DIM, HEAD_DIM), HEAD_DIM)
        dk[:, columns] = ref[:, :HEAD_DIM]
        dv[:, columns] = ref[:, HEAD_DIM:]


def place_rows(heads, *refs):
    ins, out, sem = refs[:heads], refs[heads], refs[heads + 1]
    me = lax.axis_index("head")
    width = ins[0].shape[1]
    copies = []
    for i in range(heads):
        columns = pl.ds(pl.multiple_of((me ^ i) * width, width), width)
        copies.append(pltpu.make_async_copy(ins[i], out.at[:, columns], sem.at[i]))
    for copy in copies:
        copy.start()
    for copy in copies:
        copy.wait()


def local(queries, keys, values, grad_out, block_order):
    heads, inner, outer = (lax.axis_size(n) for n in ("head", "inner", "outer"))
    block = queries.shape[0]
    chunk = inner * outer * block
    bf16 = jnp.bfloat16
    V, A = pltpu.VMEM, pl.ANY
    width = GROUP * HEAD_DIM
    dma = pltpu.SemaphoreType.DMA
    pair = 2 * HEAD_DIM

    H = pltpu.HBM
    kv_packed = call(
        functools.partial(pack, heads, 2),
        [((block, pair), bf16, V)] * heads, [(keys, H), (values, H)], [dma((heads, 2))],
    )
    kv_packed, queries, grad_out = lax.optimization_barrier((kv_packed, queries, grad_out))
    *qg_packed, block_order = call(
        functools.partial(pack, heads, 3),
        [((2, block, width), bf16, V)] * heads + [(block_order.shape, block_order.dtype, V)],
        [(queries, H), (grad_out, H), (block_order, H)],
        [dma((heads + 1, 2))],
    )
    far_first = list(reversed(range(1, heads)))
    kv_got = trade(kv_packed, "head", far_first)
    kv_got, qg_packed = lax.optimization_barrier((kv_got, qg_packed))
    qg = [qg_packed[0]] + [exchange(qg_packed[i], "head", i) for i in range(1, heads - 1)]
    last, qg = lax.optimization_barrier((qg_packed[-1], qg))
    qg.append(exchange(last, "head", heads - 1))
    mine = call(
        functools.partial(join_kv), [((heads * block, pair), bf16, V)], [(x, V) for x in kv_got]
    )[0]
    same = [mine] + [exchange(mine, "inner", s) for s in range(1, inner)]
    bundles = list(same)
    early, _ = lax.optimization_barrier((mine, qg[1:-1]))
    for e in range(1, outer):
        bundles += [exchange(x, "outer", e) for x in [early] + same[1:]]

    rows_now = GROUP * block if chunk <= 512 else GROUP * block // 2
    shares, query_grads = attend(qg, bundles, block_order, rows_now)
    core_parts = [shares[0]] + [exchange(x, "outer", e + 1) for e, x in enumerate(shares[1:])]
    sums = call(
        functools.partial(sum_cores, outer),
        [((heads * block, pair), bf16, V)] * inner,
        [(x, V) for x in core_parts],
    )
    inner_parts = [sums[0]] + [exchange(sums[s], "inner", s) for s in range(1, inner)]
    dq_parts = query_grads(sums)
    dq_got = [dq_parts[0]] + [exchange(dq_parts[i], "head", i) for i in range(1, heads)]
    back = call(
        functools.partial(sum_inner, inner),
        [((block, pair), bf16, V)] * heads,
        [(x, V) for x in inner_parts],
    )
    back_got = trade(back, "head", far_first)
    query_back = call(
        functools.partial(place_rows, heads),
        [(queries.shape, bf16, A)], [(x, V) for x in dq_got], [dma((heads,))],
    )[0]
    key_back, value_back = call(
        functools.partial(place_kv, heads),
        [(keys.shape, bf16, None)] * 2, [(x, V) for x in back_got],
    )
    return query_back, key_back, value_back


def solution(mesh):
    rows = P(("head", "inner", "outer"), None)
    return jax.shard_map(
        local, mesh=mesh, in_specs=(rows,) * 4 + (P(),), out_specs=(rows,) * 3, check_vma=False
    )
```

```python
import functools

import jax
import jax.numpy as jnp
from jax import lax
from jax.experimental import pallas as pl
from jax.experimental.pallas import tpu as pltpu
from jax.sharding import PartitionSpec as P

HEADS = 32
KV_HEADS = 4
HEAD_DIM = 128
GROUP = HEADS // KV_HEADS
SCALE = HEAD_DIM ** (-0.5)
LOG2E = 1.4426950408889634
masked_score = -1e30

NT = (((1,), (1,)), ((), ()))
NN = (((1,), (0,)), ((), ()))


def dot(a, b, dims):
    return lax.dot_general(a, b, dims, preferred_element_type=jnp.float32)


def exchange(array, axis, by):
    length = lax.axis_size(axis)
    return lax.ppermute(array, axis, [(i, i ^ by) for i in range(length)])


def trade(pieces, axis, order=None):
    got = list(pieces)
    for i in order or range(1, len(pieces)):
        got[i] = exchange(pieces[i], axis, i)
    return got


def call(body, outs, args, scratch=(), limit=16):
    arrays, in_specs = [], []
    for array, where in args:
        if where in (pltpu.VMEM, pltpu.HBM):
            array = pltpu.with_memory_space_constraint(array, where)
        arrays.append(array)
        in_specs.append(pl.BlockSpec(memory_space=pltpu.VMEM if where is None else where))
    shapes, out_specs = [], []
    for dims, dtype, where in outs:
        pinned = where is pltpu.VMEM
        shapes.append(pltpu.VMEM(dims, dtype) if pinned else jax.ShapeDtypeStruct(dims, dtype))
        out_specs.append(pl.BlockSpec(memory_space=pltpu.VMEM if where is None else where))
    return pl.pallas_call(
        body,
        out_shape=shapes,
        in_specs=in_specs,
        out_specs=out_specs,
        scratch_shapes=list(scratch),
        compiler_params=pltpu.CompilerParams(vmem_limit_bytes=limit * 1024 * 1024),
    )(*arrays)


def pack(heads, count, *refs):
    ins, outs, sem = refs[:count], refs[count:-1], refs[-1]
    me = lax.axis_index("head")
    width = ins[0].shape[1] // heads
    copies = []
    for i, out in enumerate(outs[:heads]):
        columns = pl.ds(pl.multiple_of((me ^ i) * width, width), width)
        for j, ref in enumerate(ins[:2]):
            part = out.at[j] if len(out.shape) == 3 else out.at[:, j * width : (j + 1) * width]
            copies.append(pltpu.make_async_copy(ref.at[:, columns], part, sem.at[i, j]))
    for n, (ref, out) in enumerate(zip(ins[2:], outs[heads:])):
        copies.append(pltpu.make_async_copy(ref, out, sem.at[heads + n, 0]))
    for copy in copies:
        copy.start()
    for copy in copies:
        copy.wait()


def join_kv(*refs):
    out = refs[-1]
    me = lax.axis_index("head")
    rows = refs[0].shape[0]
    for i, ref in enumerate(refs[:-1]):
        out[pl.ds(pl.multiple_of((me ^ i) * rows, rows), rows), :] = ref[...]


def main_body(heads, inner, outer, rows_now, late, order_ref, *refs):
    it = iter(refs)
    qg = [next(it) for _ in range(heads)]
    bundles = [[next(it) for _ in range(inner)] for _ in range(outer)]
    same_out = next(it)
    other_outs = [next(it) for _ in range(outer - 1)]
    if late:
        ds_out, keys, level_ref = next(it), next(it), next(it)
        values, queries, grads, s_ref, p_ref, dk_ref, dv_ref = it
    else:
        ds_out, dq_outs = None, [next(it) for _ in range(heads)]
        values, queries, grads, s_ref, p_ref, dk_ref, dv_ref, keys, key_t, dq_ref = it

    block = qg[0].shape[1]
    ranks = inner * outer
    chunk = ranks * block
    me = lax.axis_index("head")
    z = lax.axis_index("inner")
    o = lax.axis_index("outer")
    rank = z * outer + o

    for e in range(outer):
        for s in range(inner):
            other = (z ^ s) * outer + (o ^ e)
            for a in range(heads):
                at = pl.ds(pl.multiple_of(order_ref[a * ranks + other] * block, block), block)
                keys[at, :] = bundles[e][s][a * block : (a + 1) * block, :HEAD_DIM]
                values[at, :] = bundles[e][s][a * block : (a + 1) * block, HEAD_DIM:]

    place = [order_ref[(me ^ i) * ranks + rank] for i in range(heads)]
    level_of = [p // ranks for p in place]
    for i in range(heads):
        for g in range(GROUP):
            rows = slice(g * block, (g + 1) * block)
            cols = slice(g * HEAD_DIM, (g + 1) * HEAD_DIM)
            queries[level_of[i], rows, :] = qg[i][0, :, cols]
            grads[level_of[i], rows, :] = qg[i][1, :, cols]

    if not late:
        for c in range(heads):
            key_t[:, c * chunk : (c + 1) * chunk] = keys[c * chunk : (c + 1) * chunk, :].T

    all_rows = GROUP * block
    if rows_now < all_rows:
        dk_ref[...] = jnp.zeros_like(dk_ref)
        dv_ref[...] = jnp.zeros_like(dv_ref)
    for level in reversed(range(heads)):
        position = sum(jnp.where(level_of[i] == level, place[i], 0) for i in range(heads))
        shift = position * block - level * chunk

        def visit(r, level=level, shift=shift):
            here = pl.ds(pl.multiple_of(r * rows_now, rows_now), rows_now)
            q = queries[level, here, :]
            g = grads[level, here, :]
            g_t = g.T
            top = None
            for c in range(level + 1):
                span = slice(c * chunk, (c + 1) * chunk)
                s = dot(keys[span, :], q, NT)
                if c == level:
                    u = lax.broadcasted_iota(jnp.int32, s.shape, 0)
                    t = lax.broadcasted_iota(jnp.int32, s.shape, 1) % block
                    s = jnp.where(u <= t + shift, s, masked_score)
                s_ref[span, :] = s
                now = jnp.max(s, axis=0, keepdims=True)
                top = now if top is None else jnp.maximum(top, now)
            total, dots = None, None
            for c in range(level + 1):
                span = slice(c * chunk, (c + 1) * chunk)
                e = jnp.exp2((s_ref[span, :] - top) * (SCALE * LOG2E))
                s_ref[span, :] = e
                now = jnp.sum(e, axis=0, keepdims=True)
                total = now if total is None else total + now
                dp = dot(values[span, :], g, NT)
                p_ref[span, :] = dp.astype(jnp.bfloat16)
                now = jnp.sum(e * dp, axis=0, keepdims=True)
                dots = now if dots is None else dots + now
            inverse = 1.0 / total
            dots = dots * inverse
            dq = None
            for c in range(level + 1):
                span = slice(c * chunk, (c + 1) * chunk)
                p = s_ref[span, :] * inverse
                first = level == heads - 1 and rows_now == all_rows
                part = dot(g_t, p.astype(jnp.bfloat16), NT).T
                dv_ref[span, :] = part if first else dv_ref[span, :] + part
                ds = (p * (p_ref[span, :].astype(jnp.float32) - dots)).astype(jnp.bfloat16)
                part = dot(ds, q, NN)
                dk_ref[span, :] = part if first else dk_ref[span, :] + part
                if ds_out is not None:
                    ds_out[level * (level + 1) // 2 + c] = ds
                    continue
                part = dot(key_t[:, span], ds, NN)
                dq = part if dq is None else dq + part
            if ds_out is None:
                dq_ref[level, here, :] = (dq * SCALE).T.astype(jnp.bfloat16)

        if all_rows == rows_now:
            visit(0)
        else:
            pl.loop(0, all_rows // rows_now)(visit)

    if late:
        for i in range(heads):
            level_ref[i] = jnp.full(level_ref.shape[1:], level_of[i], jnp.int32)
    else:
        hand_out(dq_outs, dq_ref, level_of)
    for e in range(outer):
        out = same_out if e == 0 else other_outs[e - 1]
        for s in range(inner):
            other = (z ^ s) * outer + (o ^ e)
            for a in range(heads):
                at = pl.ds(pl.multiple_of(order_ref[a * ranks + other] * block, block), block)
                rows = slice((s * heads + a) * block, (s * heads + a + 1) * block)
                out[rows, :HEAD_DIM] = dk_ref[at, :].astype(out.dtype)
                out[rows, HEAD_DIM:] = dv_ref[at, :].astype(out.dtype)


def hand_out(dq_outs, dq_ref, level_of):
    block = dq_outs[0].shape[0]
    for out, level in zip(dq_outs, level_of):
        for g in range(GROUP):
            out[:, g * HEAD_DIM : (g + 1) * HEAD_DIM] = dq_ref[level, g * block : (g + 1) * block, :]


def query_body(heads, ds_ref, keys, level_ref, *dq_outs):
    chunk = ds_ref.shape[1]
    block = dq_outs[0].shape[0]
    by_level = []
    key_t = [keys[c * chunk : (c + 1) * chunk, :].T for c in range(heads)]
    for level in range(heads):
        dq = None
        for c in range(level + 1):
            ds = ds_ref[level * (level + 1) // 2 + c]
            part = dot(key_t[c], ds, NN)
            dq = part if dq is None else dq + part
        by_level.append((dq * SCALE).T)
    for i, out in enumerate(dq_outs):
        for g in range(GROUP):
            rows = slice(g * block, (g + 1) * block)
            piece = by_level[0][rows, :]
            for level in range(1, heads):
                piece = jnp.where(level_ref[i] == level, by_level[level][rows, :], piece)
            out[:, g * HEAD_DIM : (g + 1) * HEAD_DIM] = piece.astype(out.dtype)


def attend(qg, bundles, block_order, rows_now):
    heads, inner, outer = (lax.axis_size(n) for n in ("head", "inner", "outer"))
    block = qg[0].shape[1]
    chunk = inner * outer * block
    tokens = heads * chunk
    rows = GROUP * block
    steps = heads * (heads + 1) // 2
    bf16, f32, V = jnp.bfloat16, jnp.float32, pltpu.VMEM
    late = rows_now == rows
    dq_outs = [((block, GROUP * HEAD_DIM), bf16, V)] * heads
    outs = [((inner * heads * block, 2 * HEAD_DIM), bf16, V)] * outer
    kept = [
        ((steps, chunk, rows), bf16, V), ((tokens, HEAD_DIM), bf16, V), ((heads, block, HEAD_DIM), jnp.int32, V)
    ]
    scratch = [
        V((tokens, HEAD_DIM), bf16),
        V((heads, rows, HEAD_DIM), bf16), V((heads, rows, HEAD_DIM), bf16),
        V((tokens, rows_now), f32), V((tokens, rows_now), bf16),
        V((tokens, HEAD_DIM), f32), V((tokens, HEAD_DIM), f32),
    ]
    results = call(
        functools.partial(main_body, heads, inner, outer, rows_now, late),
        outs + (kept if late else dq_outs),
        [(block_order, pltpu.SMEM)] + [(x, V) for x in qg + bundles],
        scratch + ([] if late else [
            V((tokens, HEAD_DIM), bf16), V((HEAD_DIM, tokens), bf16), V((heads, rows, HEAD_DIM), bf16)
        ]),
        limit=24 if tokens <= 2048 else 44,
    )
    if not late:
        return results[:outer], lambda *after: results[outer:]

    def query_grads(*after):
        (ds, *others), _ = lax.optimization_barrier((results[outer:], after))
        return call(
            functools.partial(query_body, heads), dq_outs, [(x, V) for x in (ds, *others)]
        )

    return results[:outer], query_grads


def sum_cores(parts, *refs):
    ins, outs = refs[:parts], refs[parts:]
    rows = outs[0].shape[0]
    for s, out in enumerate(outs):
        span = slice(s * rows, (s + 1) * rows)
        total = ins[0][span, :].astype(jnp.float32)
        for ref in ins[1:]:
            total = total + ref[span, :].astype(jnp.float32)
        out[...] = total.astype(out.dtype)


def sum_inner(parts, *refs):
    ins, outs = refs[:parts], refs[parts:]
    me = lax.axis_index("head")
    rows = outs[0].shape[0]
    for i, out in enumerate(outs):
        at = pl.ds(pl.multiple_of((me ^ i) * rows, rows), rows)
        total = ins[0][at, :].astype(jnp.float32)
        for ref in ins[1:]:
            total = total + ref[at, :].astype(jnp.float32)
        out[:, :HEAD_DIM] = (total[:, :HEAD_DIM] * SCALE).astype(out.dtype)
        out[:, HEAD_DIM:] = total[:, HEAD_DIM:].astype(out.dtype)


def place_kv(heads, *refs):
    ins, (dk, dv) = refs[:heads], refs[heads:]
    me = lax.axis_index("head")
    for i, ref in enumerate(ins):
        columns = pl.ds(pl.multiple_of((me ^ i) * HEAD_DIM, HEAD_DIM), HEAD_DIM)
        dk[:, columns] = ref[:, :HEAD_DIM]
        dv[:, columns] = ref[:, HEAD_DIM:]


def place_rows(heads, *refs):
    ins, out, sem = refs[:heads], refs[heads], refs[heads + 1]
    me = lax.axis_index("head")
    width = ins[0].shape[1]
    copies = []
    for i in range(heads):
        columns = pl.ds(pl.multiple_of((me ^ i) * width, width), width)
        copies.append(pltpu.make_async_copy(ins[i], out.at[:, columns], sem.at[i]))
    for copy in copies:
        copy.start()
    for copy in copies:
        copy.wait()


def local(queries, keys, values, grad_out, block_order):
    heads, inner, outer = (lax.axis_size(n) for n in ("head", "inner", "outer"))
    block = queries.shape[0]
    chunk = inner * outer * block
    bf16 = jnp.bfloat16
    V, A = pltpu.VMEM, pl.ANY
    width = GROUP * HEAD_DIM
    dma = pltpu.SemaphoreType.DMA
    pair = 2 * HEAD_DIM

    H = pltpu.HBM
    kv_packed = call(
        functools.partial(pack, heads, 2),
        [((block, pair), bf16, V)] * heads, [(keys, H), (values, H)], [dma((heads, 2))],
    )
    kv_packed, queries, grad_out = lax.optimization_barrier((kv_packed, queries, grad_out))
    *qg_packed, block_order = call(
        functools.partial(pack, heads, 3),
        [((2, block, width), bf16, V)] * heads + [(block_order.shape, block_order.dtype, V)],
        [(queries, H), (grad_out, H), (block_order, H)],
        [dma((heads + 1, 2))],
    )
    far_first = list(reversed(range(1, heads)))
    kv_got = trade(kv_packed, "head", far_first)
    kv_got, qg_packed = lax.optimization_barrier((kv_got, qg_packed))
    qg = [qg_packed[0]] + [exchange(qg_packed[i], "head", i) for i in range(1, heads - 1)]
    last, qg = lax.optimization_barrier((qg_packed[-1], qg))
    qg.append(exchange(last, "head", heads - 1))
    mine = call(
        functools.partial(join_kv), [((heads * block, pair), bf16, V)], [(x, V) for x in kv_got]
    )[0]
    same = [mine] + [exchange(mine, "inner", s) for s in range(1, inner)]
    bundles = list(same)
    early, _ = lax.optimization_barrier((mine, qg[1:-1]))
    for e in range(1, outer):
        bundles += [exchange(x, "outer", e) for x in [early] + same[1:]]

    rows_now = GROUP * block if chunk <= 512 else GROUP * block // 2
    shares, query_grads = attend(qg, bundles, block_order, rows_now)
    core_parts = [shares[0]] + [exchange(x, "outer", e + 1) for e, x in enumerate(shares[1:])]
    sums = call(
        functools.partial(sum_cores, outer),
        [((heads * block, pair), bf16, V)] * inner,
        [(x, V) for x in core_parts],
    )
    inner_parts = [sums[0]] + [exchange(sums[s], "inner", s) for s in range(1, inner)]
    dq_parts = query_grads(sums)
    dq_got = [dq_parts[0]] + [exchange(dq_parts[i], "head", i) for i in range(1, heads)]
    back = call(
        functools.partial(sum_inner, inner),
        [((block, pair), bf16, V)] * heads,
        [(x, V) for x in inner_parts],
    )
    back_got = trade(back, "head", far_first)
    query_back = call(
        functools.partial(place_rows, heads),
        [(queries.shape, bf16, A)], [(x, V) for x in dq_got], [dma((heads,))],
    )[0]
    key_back, value_back = call(
        functools.partial(place_kv, heads),
        [(keys.shape, bf16, None)] * 2, [(x, V) for x in back_got],
    )
    return query_back, key_back, value_back


def solution(mesh):
    rows = P(("head", "inner", "outer"), None)
    return jax.shard_map(
        local, mesh=mesh, in_specs=(rows,) * 4 + (P(),), out_specs=(rows,) * 3, check_vma=False
    )
```
